32 devices in a mesh: groups: 2 (over x), tensor: 8 (over z, y), seq: 2 (over core).
Axes of the slice: x: 2, y: 2, z: 4, core: 2. Of those that a mesh axis runs over, the one named last changes fastest.
Arguments:
- tokens: bfloat16 [1024, 4096], P(('groups', 'tensor'), 'seq'), parts along dimension 0, may hold values from -6 to 6
- gate_weight: bfloat16 [4096, 16384], P('seq', 'tensor'), may hold values from -0.125 to 0.125
- up_weight: bfloat16 [4096, 16384], P('seq', 'tensor'), may hold values from -0.125 to 0.125
- down_weight: bfloat16 [16384, 4096], P('tensor', 'seq'), may hold values from -0.125 to 0.125
- gate_mask: int32 [32, 128], P('seq', 'tensor'), may hold values from 0 to 1, as said below
- up_mask: int32 [32, 128], P('seq', 'tensor'), may hold values from 0 to 1, as said below
- down_mask: int32 [128, 32], P('tensor', 'seq'), may hold values from 0 to 1, as said below
Outputs:
- mixed: bfloat16 [1024, 4096], P(('groups', 'tensor'), 'seq'), parts along dimension 0
The draws below stay inside these ranges and needn't reach their ends.
There are 2 independent parts, one for each index of `groups`. The reference program is written for one: setup_inputs(seed, part) draws one part's arguments, and reference() takes and returns one part's arrays. A program takes and returns all parts, laid end to end along the dimension named above; an argument that names none is the same for every part. Nothing has to cross between parts.
Inputs may be any that keep to these rules, and one draw needn't show every extreme that they name: `gate_mask`: 1 keeps a 128 x 128 block of the weight, 0 removes it; the share of kept blocks varies from one block of hidden units to another. `up_mask`: as gate_mask. `down_mask`: as gate_mask, with hidden units along the first dimension.
All inputs are finite; a program needn't handle non-finite values.
Results may differ from the reference program's by a relative error of at most 0.005.
Values may be sent and summed in bfloat16 or wider, within the bound.
No kernel may reach another device: no remote copies, remote signals or barrier semaphores. Data moves between devices by JAX's collectives and lax.ppermute only.
A program may use at most 128 MiB of HBM per device.

```python
import jax
import jax.numpy as jnp

BLOCK = 128
D = 4096
FF = 16384
TOKENS = 512


def block_levels(key):
    return jax.random.randint(key, (FF // BLOCK,), 1, 8)


def draw_gate_mask(key, part):
    levels = block_levels(key)
    key = jax.random.fold_in(key, 11)
    raw = jax.random.randint(key, (D // BLOCK, FF // BLOCK), 0, 8)
    return (raw < levels[None, :]).astype(jnp.int32)


def draw_up_mask(key, part):
    levels = block_levels(key)
    key = jax.random.fold_in(key, 12)
    raw = jax.random.randint(key, (D // BLOCK, FF // BLOCK), 0, 8)
    return (raw < levels[None, :]).astype(jnp.int32)


def draw_down_mask(key, part):
    levels = block_levels(key)
    key = jax.random.fold_in(key, 13)
    raw = jax.random.randint(key, (FF // BLOCK, D // BLOCK), 0, 8)
    return (raw < levels[:, None]).astype(jnp.int32)


def shard_levels(stream_key, shape, cuts, least, top_value):
    def one(dim, parts):
        steps = jax.random.uniform(jax.random.fold_in(jax.random.fold_in(stream_key, 6), dim), (parts,), jnp.float32, least / len(cuts), top_value / len(cuts))
        return jnp.repeat(jnp.exp(steps), shape[dim] // parts).reshape((-1,) + (1,) * (len(shape) - dim - 1))

    gain = one(*cuts[0])
    for cut in cuts[1:]:
        gain = gain * one(*cut)
    return gain


def noise(own_key, shape, spread, bound, split=(), kind=jnp.bfloat16):
    drawn = spread * jax.random.normal(own_key, shape, jnp.float32)
    if split:
        drawn = drawn * shard_levels(own_key, shape, split, -0.22, 0.18)
    return jnp.clip(drawn, -bound, bound).astype(kind)


def setup_inputs(seed: int = 0, part: int = 0) -> dict:
    seeds = jax.random.split(jax.random.key(seed), 8)
    own_keys = jax.random.split(jax.random.fold_in(seeds[7], part), 8)
    tokens = noise(own_keys[0], (TOKENS, D), 1.0, 6.0, ((0, 8), (1, 2)))
    gate_weight = noise(seeds[1], (D, FF), (D // 2) ** -0.5, 0.125, ((0, 2), (1, 8)))
    up_weight = noise(seeds[2], (D, FF), (D // 2) ** -0.5, 0.125, ((0, 2), (1, 8)))
    down_weight = noise(seeds[3], (FF, D), (FF // 8) ** -0.5, 0.125, ((0, 8), (1, 2)))
    gate_mask = draw_gate_mask(jax.random.fold_in(seeds[7], 71), part)
    up_mask = draw_up_mask(jax.random.fold_in(seeds[7], 71), part)
    down_mask = draw_down_mask(jax.random.fold_in(seeds[7], 71), part)
    return {"tokens": tokens, "gate_weight": gate_weight, "up_weight": up_weight, "down_weight": down_weight, "gate_mask": gate_mask, "up_mask": up_mask, "down_mask": down_mask}


def pruned(weight, mask):
    rows, cols = weight.shape
    shaped = weight.reshape(rows // BLOCK, BLOCK, cols // BLOCK, BLOCK)
    kept = shaped * mask.astype(jnp.bfloat16)[:, None, :, None]
    return kept.reshape(rows, cols)


def reference(tokens, gate_weight, up_weight, down_weight, gate_mask, up_mask, down_mask):
    gate_pruned = pruned(gate_weight, gate_mask)
    up_pruned = pruned(up_weight, up_mask)
    down_pruned = pruned(down_weight, down_mask)
    gate = jnp.dot(tokens, gate_pruned, preferred_element_type=jnp.float32)
    up = jnp.dot(tokens, up_pruned, preferred_element_type=jnp.float32)
    hidden = (jax.nn.silu(gate) * up).astype(jnp.bfloat16)
    return jnp.dot(hidden, down_pruned, preferred_element_type=jnp.float32).astype(jnp.bfloat16)
```

```python
import jax
import jax.numpy as jnp
from jax import lax
from jax.sharding import PartitionSpec as P

BLOCK = 128
BF16 = jnp.bfloat16
F32 = jnp.float32


def pruned(weight, mask):
    rows, cols = weight.shape
    shaped = weight.reshape(rows // BLOCK, BLOCK, cols // BLOCK, BLOCK)
    kept = shaped * mask.astype(BF16)[:, None, :, None]
    return kept.reshape(rows, cols)


def dot(a, b):
    return jnp.dot(a, b, preferred_element_type=F32)


def plain(tokens, gate_weight, up_weight, down_weight, gate_mask, up_mask, down_mask):
    gathered = lax.all_gather(tokens, "tensor", axis=0, tiled=True)
    gate_part = dot(gathered, pruned(gate_weight, gate_mask))
    up_part = dot(gathered, pruned(up_weight, up_mask))
    gate = lax.psum_scatter(gate_part, "seq", scatter_dimension=0, tiled=True)
    up = lax.psum_scatter(up_part, "seq", scatter_dimension=0, tiled=True)
    hidden = (jax.nn.silu(gate) * up).astype(BF16)
    full_hidden = lax.all_gather(hidden, "seq", axis=0, tiled=True)
    return lax.psum_scatter(
        dot(full_hidden, pruned(down_weight, down_mask)), "tensor", scatter_dimension=0, tiled=True
    ).astype(BF16)


ACROSS = [(2 * z + y, 2 * z + 1 - y) for z in range(4) for y in range(2)]
PAIR = [(2 * z + y, 2 * (z ^ 1) + y) for z in range(4) for y in range(2)]
MIDDLE = [(2 * z + y, 2 * (3 - z) + y) for z in (1, 2) for y in range(2)]
OUTWARD = [(2 * z + y, 2 * (z ^ 1) + y) for z in (1, 2) for y in range(2)]
INWARD = [(2 * z + y, 2 * (z ^ 1) + y) for z in (0, 3) for y in range(2)]


def move(value, perm):
    return lax.ppermute(value, "tensor", perm)


def inner():
    z = lax.axis_index("tensor") // 2
    return (z == 1) | (z == 2)


def gather(own):
    pair = move(own, PAIR)
    near = move(own, MIDDLE)
    own_y = move(own, ACROSS)
    far = move(pair, MIDDLE)
    near_out = move(near, OUTWARD)
    pair_y = move(pair, ACROSS)
    near = jnp.where(inner(), near, near_out)
    far_out = move(far, OUTWARD)
    near_y = move(near, ACROSS)
    far = jnp.where(inner(), far, far_out)
    far_y = move(far, ACROSS)
    return own, own_y, pair, pair_y, near, near_y, far, far_y


def add(a, b):
    return a.astype(F32) + b.astype(F32)


def scatter(own, own_y, pair, pair_y, near, near_y, far, far_y):
    far_s = add(far, move(far_y, ACROSS)).astype(BF16)
    near_s = add(near, move(near_y, ACROSS)).astype(BF16)
    pair_s = add(pair, move(pair_y, ACROSS))
    own_s = add(own, move(own_y, ACROSS))
    far_s = add(far_s, move(far_s, INWARD)).astype(BF16)
    near_s = add(near_s, move(near_s, INWARD)).astype(BF16)
    pair_s = add(pair_s, move(far_s, MIDDLE)).astype(BF16)
    own_s = add(own_s, move(near_s, MIDDLE))
    return add(own_s, move(pair_s, PAIR)).astype(BF16)


SWAP = [(0, 1), (1, 0)]


def lined(tokens, gate_weight, up_weight, down_weight, gate_mask, up_mask, down_mask):
    rows = tokens.shape[0]
    half = rows // 2
    gate_pruned, up_pruned, down_pruned = lax.optimization_barrier(
        (pruned(gate_weight, gate_mask), pruned(up_weight, up_mask), pruned(down_weight, down_mask))
    )
    core = lax.axis_index("seq")
    gathered = jnp.stack(gather(tokens)).reshape(8, 2, half, -1)
    theirs = lax.dynamic_index_in_dim(gathered, 1 - core, 1, keepdims=False).reshape(8 * half, -1)
    mine = lax.dynamic_index_in_dim(gathered, core, 1, keepdims=False).reshape(8 * half, -1)
    gate_sent = lax.ppermute(dot(theirs, gate_pruned).astype(BF16), "seq", SWAP)
    up_sent = lax.ppermute(dot(theirs, up_pruned).astype(BF16), "seq", SWAP)
    gate = dot(mine, gate_pruned) + gate_sent.astype(F32)
    up = dot(mine, up_pruned) + up_sent.astype(F32)
    hidden = (jax.nn.silu(gate) * up).astype(BF16)
    other = lax.ppermute(hidden, "seq", SWAP)
    parts_mine = dot(hidden, down_pruned).astype(BF16).reshape(8, half, -1)
    parts_theirs = dot(other, down_pruned).astype(BF16).reshape(8, half, -1)
    first = jnp.where(core == 0, parts_mine, parts_theirs)
    second = jnp.where(core == 0, parts_theirs, parts_mine)
    parts = jnp.stack([first, second], axis=1).reshape(8, rows, -1)
    return scatter(*(parts[i] for i in range(8)))


def solution(mesh):
    return jax.shard_map(
        lined if mesh.shape["tensor"] == 8 and mesh.shape["seq"] == 2 else plain,
        mesh=mesh,
        in_specs=(
            P(("groups", "tensor"), "seq"),
            P("seq", "tensor"),
            P("seq", "tensor"),
            P("tensor", "seq"),
            P("seq", "tensor"),
            P("seq", "tensor"),
            P("tensor", "seq"),
        ),
        out_specs=P(("groups", "tensor"), "seq"),
        check_vma=False,
    )
```

```python
import jax
import jax.numpy as jnp
from jax import lax
from jax.experimental import pallas as pl
from jax.experimental.pallas import tpu as pltpu
from jax.sharding import PartitionSpec as P

BLOCK = 128
LIMIT = 16 << 20
BF16 = jnp.bfloat16
F32 = jnp.float32


def pruned(weight, mask):
    rows, cols = weight.shape
    shaped = weight.reshape(rows // BLOCK, BLOCK, cols // BLOCK, BLOCK)
    kept = shaped * mask.astype(BF16)[:, None, :, None]
    return kept.reshape(rows, cols)


def dot(a, b):
    return jnp.dot(a, b, preferred_element_type=F32)


def plain(tokens, gate_weight, up_weight, down_weight, gate_mask, up_mask, down_mask):
    gathered = lax.all_gather(tokens, "tensor", axis=0, tiled=True)
    gate_part = dot(gathered, pruned(gate_weight, gate_mask))
    up_part = dot(gathered, pruned(up_weight, up_mask))
    gate = lax.psum_scatter(gate_part, "seq", scatter_dimension=0, tiled=True)
    up = lax.psum_scatter(up_part, "seq", scatter_dimension=0, tiled=True)
    hidden = (jax.nn.silu(gate) * up).astype(BF16)
    full_hidden = lax.all_gather(hidden, "seq", axis=0, tiled=True)
    return lax.psum_scatter(
        dot(full_hidden, pruned(down_weight, down_mask)), "tensor", scatter_dimension=0, tiled=True
    ).astype(BF16)


ACROSS = [(2 * z + y, 2 * z + 1 - y) for z in range(4) for y in range(2)]
PAIR = [(2 * z + y, 2 * (z ^ 1) + y) for z in range(4) for y in range(2)]
MIDDLE = [(2 * z + y, 2 * (3 - z) + y) for z in (1, 2) for y in range(2)]
OUTWARD = [(2 * z + y, 2 * (z ^ 1) + y) for z in (1, 2) for y in range(2)]
INWARD = [(2 * z + y, 2 * (z ^ 1) + y) for z in (0, 3) for y in range(2)]


def move(value, perm):
    return lax.ppermute(value, "tensor", perm)


def inner():
    z = lax.axis_index("tensor") // 2
    return (z == 1) | (z == 2)


def after(value, *others):
    return lax.optimization_barrier((value, *others))[0]


def gather(own, early):
    pair = move(own, PAIR)
    near = move(own, MIDDLE)
    own_y = move(own, ACROSS)
    far = move(pair, MIDDLE)
    near_out = move(near, OUTWARD)
    pair_y = move(after(pair, own_y), ACROSS)
    near = jnp.where(inner(), near, near_out)
    far_out = move(far, OUTWARD)
    near_y = move(after(near, pair_y), ACROSS)
    far = jnp.where(inner(), far, far_out)
    sums = early((own, own_y, pair, pair_y))
    far, near_y, *sums = lax.optimization_barrier((far, near_y, *sums))
    far_y = move(far, ACROSS)
    return sums, (near, near_y, far, far_y)


def add(a, b):
    return a.astype(F32) + b.astype(F32)


def scatter(own, own_y, pair, pair_y, near, near_y, far, far_y):
    far_s = add(far, move(far_y, ACROSS)).astype(BF16)
    near_s = add(near, move(near_y, ACROSS)).astype(BF16)
    pair_s = add(pair, move(pair_y, ACROSS))
    own_s = add(own, move(own_y, ACROSS))
    far_s = add(far_s, move(far_s, INWARD)).astype(BF16)
    near_s = add(near_s, move(near_s, INWARD)).astype(BF16)
    pair_s = add(pair_s, move(far_s, MIDDLE)).astype(BF16)
    own_s = add(own_s, move(near_s, MIDDLE))
    return add(own_s, move(pair_s, PAIR)).astype(BF16)


SWAP = [(0, 1), (1, 0)]
WHOLE = pl.BlockSpec(memory_space=pltpu.VMEM)
SCALAR = pl.BlockSpec(memory_space=pltpu.SMEM)
IN_HBM = pl.BlockSpec(memory_space=pltpu.HBM)
PIECES = 8
TILE = 512


def swap(value):
    return lax.ppermute(value, "seq", SWAP)


def prune_kernel(mask, weight, out, arrived):
    rows = out.shape[0] // PIECES
    copies = [
        pltpu.make_async_copy(
            weight.at[pl.ds(i * rows, rows), :], out.at[pl.ds(i * rows, rows), :], arrived.at[i]
        )
        for i in range(PIECES)
    ]
    for copy in copies:
        copy.start()
    for i, copy in enumerate(copies):
        copy.wait()
        for k in range(rows // BLOCK):
            at = i * rows + k * BLOCK

            @pl.loop(0, out.shape[1] // BLOCK)
            def _(j):
                @pl.when(mask[at // BLOCK, j] == 0)
                def _():
                    columns = pl.ds(pl.multiple_of(j * BLOCK, BLOCK), BLOCK)
                    out[at : at + BLOCK, columns] = jnp.zeros((BLOCK, BLOCK), BF16)


def prune(weight, mask):
    return pl.pallas_call(
        prune_kernel,
        out_shape=pltpu.VMEM(weight.shape, BF16),
        in_specs=[SCALAR, IN_HBM],
        out_specs=WHOLE,
        scratch_shapes=[pltpu.SemaphoreType.DMA((PIECES,))],
        compiler_params=pltpu.CompilerParams(vmem_limit_bytes=LIMIT),
        cost_estimate=pl.CostEstimate(flops=0, bytes_accessed=2 * weight.size, transcendentals=0),
        name="prune",
    )(mask, pltpu.with_memory_space_constraint(weight, pltpu.HBM))


def partial_kernel(core, *refs):
    *blocks, gate_w, up_w, theirs, mine, lhs = refs
    rows = blocks[0].shape[0]
    half = len(blocks) // 2
    for i, block in enumerate(blocks):
        side = core[0] if i < half else 1 - core[0]
        at = pl.multiple_of((1 - side) * half * rows + (i % half) * rows, rows)
        lhs[pl.ds(at, rows), :] = block[...]

    for which, weight in enumerate((gate_w, up_w)):

        @pl.loop(0, weight.shape[1] // TILE)
        def _(j):
            columns = pl.ds(pl.multiple_of(j * TILE, TILE), TILE)
            sums = dot(lhs[...], weight[:, columns])
            theirs[which, :, columns] = sums[: half * rows]
            mine[which, :, columns] = sums[half * rows :]


def partials(core, blocks, gate_w, up_w):
    rows = blocks[0].shape[0] * len(blocks)
    depth, width = gate_w.shape
    out = jax.ShapeDtypeStruct((2, rows // 2, width), F32)
    return pl.pallas_call(
        partial_kernel,
        out_shape=[out, out],
        in_specs=[SCALAR] + [WHOLE] * (len(blocks) + 2),
        out_specs=[WHOLE, WHOLE],
        scratch_shapes=[pltpu.VMEM((rows, depth), BF16)],
        compiler_params=pltpu.CompilerParams(vmem_limit_bytes=LIMIT),
        cost_estimate=pl.CostEstimate(flops=4 * rows * depth * width, bytes_accessed=2 * rows * depth, transcendentals=0),
        name="partials",
    )(core, *blocks, gate_w, up_w)


def down_kernel(core, mine, theirs, weight, *refs):
    outs, lhs = refs[:-1], refs[-1]
    rows = outs[0].shape[0]
    half = mine.shape[0]
    lhs[pl.ds(pl.multiple_of(core[0] * half, half), half), :] = mine[...]
    lhs[pl.ds(pl.multiple_of((1 - core[0]) * half, half), half), :] = theirs[...]

    @pl.loop(0, weight.shape[1] // TILE)
    def _(j):
        columns = pl.ds(pl.multiple_of(j * TILE, TILE), TILE)
        sums = dot(lhs[...], weight[:, columns]).astype(BF16)
        for i, out in enumerate(outs):
            out[:, columns] = sums[i * rows : (i + 1) * rows, :]


def down_of(core, mine, theirs, weight, n):
    half = mine.shape[0]
    depth, width = weight.shape
    return pl.pallas_call(
        down_kernel,
        out_shape=[jax.ShapeDtypeStruct((2 * half // n, width), BF16)] * n,
        in_specs=[SCALAR, WHOLE, WHOLE, WHOLE],
        out_specs=[WHOLE] * n,
        scratch_shapes=[pltpu.VMEM((2 * half, depth), BF16)],
        compiler_params=pltpu.CompilerParams(vmem_limit_bytes=LIMIT),
        cost_estimate=pl.CostEstimate(flops=4 * half * depth * width, bytes_accessed=4 * half * depth, transcendentals=0),
        name="down",
    )(core, mine, theirs, weight)


def lined(tokens, gate_weight, up_weight, down_weight, gate_mask, up_mask, down_mask):
    core = jnp.reshape(lax.axis_index("seq"), (1,)).astype(jnp.int32)
    gate_w, up_w, down_w = prune(gate_weight, gate_mask), prune(up_weight, up_mask), prune(down_weight, down_mask)

    def hidden(theirs, mine):
        gate, up = mine + swap(theirs)
        return (jax.nn.silu(gate) * up).astype(BF16)

    (theirs, mine), blocks = gather(tokens, lambda blocks: partials(core, blocks, gate_w, up_w))
    first = hidden(theirs, mine)
    *blocks, first, down_w = lax.optimization_barrier((*blocks, first, down_w))
    first_in = swap(first)
    theirs, mine = partials(core, blocks, gate_w, up_w)
    theirs, first_in = lax.optimization_barrier((theirs, first_in))
    theirs_sent = swap(theirs)
    parts = down_of(core, first, first_in, down_w, 4)
    gate, up = mine + theirs_sent
    second = (jax.nn.silu(gate) * up).astype(BF16)
    parts += down_of(core, second, swap(second), down_w, 4)
    return scatter(*parts)


def solution(mesh):
    return jax.shard_map(
        lined if mesh.shape["tensor"] == 8 and mesh.shape["seq"] == 2 else plain,
        mesh=mesh,
        in_specs=(
            P(("groups", "tensor"), "seq"),
            P("seq", "tensor"),
            P("seq", "tensor"),
            P("tensor", "seq"),
            P("seq", "tensor"),
            P("seq", "tensor"),
            P("tensor", "seq"),
        ),
        out_specs=P(("groups", "tensor"), "seq"),
        check_vma=False,
    )
```

```python
import jax
import jax.numpy as jnp
from jax import lax
from jax.experimental import pallas as pl
from jax.experimental.pallas import tpu as pltpu
from jax.sharding import PartitionSpec as P

BLOCK = 128
LIMIT = 16 << 20
BF16 = jnp.bfloat16
F32 = jnp.float32


def pruned(weight, mask):
    rows, cols = weight.shape
    shaped = weight.reshape(rows // BLOCK, BLOCK, cols // BLOCK, BLOCK)
    kept = shaped * mask.astype(BF16)[:, None, :, None]
    return kept.reshape(rows, cols)


def dot(a, b):
    return jnp.dot(a, b, preferred_element_type=F32)


def plain(tokens, gate_weight, up_weight, down_weight, gate_mask, up_mask, down_mask):
    gathered = lax.all_gather(tokens, "tensor", axis=0, tiled=True)
    gate_part = dot(gathered, pruned(gate_weight, gate_mask))
    up_part = dot(gathered, pruned(up_weight, up_mask))
    gate = lax.psum_scatter(gate_part, "seq", scatter_dimension=0, tiled=True)
    up = lax.psum_scatter(up_part, "seq", scatter_dimension=0, tiled=True)
    hidden = (jax.nn.silu(gate) * up).astype(BF16)
    full_hidden = lax.all_gather(hidden, "seq", axis=0, tiled=True)
    return lax.psum_scatter(
        dot(full_hidden, pruned(down_weight, down_mask)), "tensor", scatter_dimension=0, tiled=True
    ).astype(BF16)


ACROSS = [(2 * z + y, 2 * z + 1 - y) for z in range(4) for y in range(2)]
PAIR = [(2 * z + y, 2 * (z ^ 1) + y) for z in range(4) for y in range(2)]
MIDDLE = [(2 * z + y, 2 * (3 - z) + y) for z in (1, 2) for y in range(2)]
OUTWARD = [(2 * z + y, 2 * (z ^ 1) + y) for z in (1, 2) for y in range(2)]
INWARD = [(2 * z + y, 2 * (z ^ 1) + y) for z in (0, 3) for y in range(2)]


def move(value, perm):
    return lax.ppermute(value, "tensor", perm)


def inner():
    z = lax.axis_index("tensor") // 2
    return (z == 1) | (z == 2)


def after(value, *others):
    return lax.optimization_barrier((value, *others))[0]


def gather(own, early):
    pair = move(own, PAIR)
    near = move(own, MIDDLE)
    own_y = move(own, ACROSS)
    far = move(pair, MIDDLE)
    near_out = move(near, OUTWARD)
    pair_y = move(after(pair, own_y), ACROSS)
    near = jnp.where(inner(), near, near_out)
    far_first = far
    far_out = move(far, OUTWARD)
    near_y = move(after(near, pair_y), ACROSS)
    far = jnp.where(inner(), far, far_out)
    sums = early((own, own_y, pair, after(pair_y, far_first)))
    far, near_y, *sums = lax.optimization_barrier((far, near_y, *sums))
    far_y = move(far, ACROSS)
    return sums, (near, near_y, far, far_y)


def add(a, b):
    return a.astype(F32) + b.astype(F32)


def scatter(own, own_y, pair, pair_y, near, near_y, far, far_y):
    far_in = move(far_y, ACROSS)
    near_in = move(near_y, ACROSS)
    pair_in = move(after(pair_y, far_in), ACROSS)
    own_in = move(after(own_y, near_in), ACROSS)
    far_s = add(far, far_in).astype(BF16)
    near_s = add(after(near, far_s), near_in).astype(BF16)
    far_s = add(far_s, move(far_s, INWARD)).astype(BF16)
    near_s = add(near_s, move(near_s, INWARD)).astype(BF16)
    pair_s = (add(pair, pair_in) + move(far_s, MIDDLE).astype(F32)).astype(BF16)
    own_s = add(own, own_in) + move(near_s, MIDDLE).astype(F32)
    return add(own_s, move(pair_s, PAIR)).astype(BF16)


SWAP = [(0, 1), (1, 0)]
WHOLE = pl.BlockSpec(memory_space=pltpu.VMEM)
SCALAR = pl.BlockSpec(memory_space=pltpu.SMEM)
IN_HBM = pl.BlockSpec(memory_space=pltpu.HBM)
PIECES = 8


def swap(value):
    return lax.ppermute(value, "seq", SWAP)


def prune_kernel(mask, weight, out, arrived):
    rows = out.shape[0] // PIECES
    copies = [
        pltpu.make_async_copy(
            weight.at[pl.ds(i * rows, rows), :], out.at[pl.ds(i * rows, rows), :], arrived.at[i]
        )
        for i in range(PIECES)
    ]
    for copy in copies:
        copy.start()
    for i, copy in enumerate(copies):
        copy.wait()
        for k in range(i * rows // BLOCK, (i + 1) * rows // BLOCK):
            for j in range(out.shape[1] // BLOCK):

                @pl.when(mask[k, j] == 0)
                def _():
                    at = (slice(k * BLOCK, (k + 1) * BLOCK), slice(j * BLOCK, (j + 1) * BLOCK))
                    out[at] = jnp.zeros((BLOCK, BLOCK), BF16)


def prune(weight, mask):
    return pl.pallas_call(
        prune_kernel,
        out_shape=pltpu.VMEM(weight.shape, BF16),
        in_specs=[SCALAR, IN_HBM],
        out_specs=WHOLE,
        scratch_shapes=[pltpu.SemaphoreType.DMA((PIECES,))],
        compiler_params=pltpu.CompilerParams(vmem_limit_bytes=LIMIT),
        cost_estimate=pl.CostEstimate(flops=0, bytes_accessed=2 * weight.size, transcendentals=0),
        name="prune",
    )(mask, pltpu.with_memory_space_constraint(weight, pltpu.HBM))


def of_core(core, first, second):
    return jnp.where(core == 0, first, second)


def lined(tokens, gate_weight, up_weight, down_weight, gate_mask, up_mask, down_mask):
    core = lax.axis_index("seq")
    weights = []

    def halves(blocks):
        n = len(blocks) // 2
        low, high = jnp.concatenate(blocks[:n]), jnp.concatenate(blocks[n:])
        return of_core(core, high, low), of_core(core, low, high)

    def early(blocks):
        gate_w = prune(gate_weight, gate_mask)
        up_w = prune(after(up_weight, blocks[1]), up_mask)
        theirs, mine = halves(blocks)
        return dot(theirs, gate_w), dot(theirs, up_w), mine, gate_w, up_w

    def hidden(mine, gate_w, up_w, gate_in, up_in):
        gate, up = dot(mine, gate_w) + gate_in, dot(mine, up_w) + up_in
        return (jax.nn.silu(gate) * up).astype(BF16)

    def down(mine, theirs, down_w, n):
        low, high = of_core(core, mine, theirs), of_core(core, theirs, mine)
        sums = dot(jnp.concatenate([low, high]), down_w).astype(BF16)
        return jnp.split(sums, n)

    (gate_out, up_out, mine, gate_w, up_w), blocks = gather(tokens, early)
    down_w = prune(after(down_weight, blocks[1]), down_mask)
    first = hidden(mine, gate_w, up_w, swap(gate_out), swap(up_out))
    *blocks, first, down_w = lax.optimization_barrier((*blocks, first, down_w))
    theirs, mine = halves(blocks)
    gate_out, up_out = dot(theirs, gate_w), dot(theirs, up_w)
    second = hidden(mine, gate_w, up_w, swap(gate_out), swap(up_out))
    parts_far = down(second, swap(second), down_w, 4)
    parts_near = down(first, swap(first), down_w, 4)
    return scatter(*parts_near, *parts_far)


def solution(mesh):
    return jax.shard_map(
        lined if mesh.shape["tensor"] == 8 and mesh.shape["seq"] == 2 else plain,
        mesh=mesh,
        in_specs=(
            P(("groups", "tensor"), "seq"),
            P("seq", "tensor"),
            P("seq", "tensor"),
            P("tensor", "seq"),
            P("seq", "tensor"),
            P("seq", "tensor"),
            P("tensor", "seq"),
        ),
        out_specs=P(("groups", "tensor"), "seq"),
        check_vma=False,
    )
```

```python
import jax
import jax.numpy as jnp
from jax import lax
from jax.experimental import pallas as pl
from jax.experimental.pallas import tpu as pltpu
from jax.sharding import PartitionSpec as P

BLOCK = 128
LIMIT = 8 << 20
BF16 = jnp.bfloat16
F32 = jnp.float32


def pruned(weight, mask):
    rows, cols = weight.shape
    shaped = weight.reshape(rows // BLOCK, BLOCK, cols // BLOCK, BLOCK)
    kept = shaped * mask.astype(BF16)[:, None, :, None]
    return kept.reshape(rows, cols)


def dot(a, b):
    return jnp.dot(a, b, preferred_element_type=F32)


def plain(tokens, gate_weight, up_weight, down_weight, gate_mask, up_mask, down_mask):
    gathered = lax.all_gather(tokens, "tensor", axis=0, tiled=True)
    gate_part = dot(gathered, pruned(gate_weight, gate_mask))
    up_part = dot(gathered, pruned(up_weight, up_mask))
    gate = lax.psum_scatter(gate_part, "seq", scatter_dimension=0, tiled=True)
    up = lax.psum_scatter(up_part, "seq", scatter_dimension=0, tiled=True)
    hidden = (jax.nn.silu(gate) * up).astype(BF16)
    full_hidden = lax.all_gather(hidden, "seq", axis=0, tiled=True)
    return lax.psum_scatter(
        dot(full_hidden, pruned(down_weight, down_mask)), "tensor", scatter_dimension=0, tiled=True
    ).astype(BF16)


ACROSS = [(2 * z + y, 2 * z + 1 - y) for z in range(4) for y in range(2)]
PAIR = [(2 * z + y, 2 * (z ^ 1) + y) for z in range(4) for y in range(2)]
MIDDLE = [(2 * z + y, 2 * (3 - z) + y) for z in (1, 2) for y in range(2)]
OUTWARD = [(2 * z + y, 2 * (z ^ 1) + y) for z in (1, 2) for y in range(2)]
INWARD = [(2 * z + y, 2 * (z ^ 1) + y) for z in (0, 3) for y in range(2)]


def move(value, perm):
    return lax.ppermute(value, "tensor", perm)


def inner():
    z = lax.axis_index("tensor") // 2
    return (z == 1) | (z == 2)


def after(value, *others):
    return lax.optimization_barrier((value, *others))[0]


def gather(own, early):
    pair = move(own, PAIR)
    near = move(own, MIDDLE)
    own_y = move(own, ACROSS)
    far = move(pair, MIDDLE)
    near_out = move(near, OUTWARD)
    pair_y = move(after(pair, own_y), ACROSS)
    near_first = near
    near = jnp.where(inner(), near, near_out)
    far_first = far
    far_out = move(far, OUTWARD)
    near_y = move(after(near, pair_y), ACROSS)
    far = jnp.where(inner(), far, far_out)
    late = dict(own_y=own_y, pair=pair, near_first=near_first, pair_y=pair_y, far_first=far_first, far_out=far_out, near_y=near_y, near=near, far=far)
    sums = early((own, own_y, pair, after(pair_y, far_out)), late)
    far, near_y, *sums = lax.optimization_barrier((far, near_y, *sums))
    far_y = move(far, ACROSS)
    return sums, (near, near_y, far, far_y)


def add(a, b):
    return a.astype(F32) + b.astype(F32)


def scatter(own, own_y, pair, pair_y, near, near_y, far, far_y):
    far_in = move(far_y, ACROSS)
    near_in = move(near_y, ACROSS)
    pair_in = move(after(pair_y, far_in), ACROSS)
    own_in = move(after(own_y, near_in), ACROSS)
    far_s = add(far, far_in).astype(BF16)
    near_s = add(after(near, far_s), near_in).astype(BF16)
    far_s = add(far_s, move(far_s, INWARD)).astype(BF16)
    near_s = add(near_s, move(near_s, INWARD)).astype(BF16)
    pair_s = (add(pair, pair_in) + move(far_s, MIDDLE).astype(F32)).astype(BF16)
    own_s = add(own, own_in) + move(near_s, MIDDLE).astype(F32)
    return add(own_s, move(pair_s, PAIR)).astype(BF16)


SWAP = [(0, 1), (1, 0)]
WHOLE = pl.BlockSpec(memory_space=pltpu.VMEM)
IN_HBM = pl.BlockSpec(memory_space=pltpu.HBM)
PIECES = 8
SCALAR = pl.BlockSpec(memory_space=pltpu.SMEM)


def swap(value):
    return lax.ppermute(value, "seq", SWAP)


def prune_kernel(mask, weight, out):
    for k in range(out.shape[0] // BLOCK):
        for j in range(out.shape[1] // BLOCK):
            at = (slice(k * BLOCK, (k + 1) * BLOCK), slice(j * BLOCK, (j + 1) * BLOCK))
            out[at] = jnp.where(mask[k, j] != 0, weight[at], jnp.zeros((BLOCK, BLOCK), BF16))


def prune(weight, mask):
    return pl.pallas_call(
        prune_kernel,
        out_shape=pltpu.VMEM(weight.shape, BF16),
        in_specs=[SCALAR, WHOLE],
        out_specs=WHOLE,
        compiler_params=pltpu.CompilerParams(vmem_limit_bytes=LIMIT),
        cost_estimate=pl.CostEstimate(flops=0, bytes_accessed=1024, transcendentals=0),
        name="prune",
    )(mask, weight)


def fetch_prune_kernel(mask, weight, out, arrived):
    rows = out.shape[0] // PIECES
    copies = [
        pltpu.make_async_copy(
            weight.at[pl.ds(i * rows, rows), :], out.at[pl.ds(i * rows, rows), :], arrived.at[i]
        )
        for i in range(PIECES)
    ]
    for copy in copies:
        copy.start()
    for i, copy in enumerate(copies):
        copy.wait()
        for k in range(i * rows // BLOCK, (i + 1) * rows // BLOCK):
            for j in range(out.shape[1] // BLOCK):

                @pl.when(mask[k, j] == 0)
                def _():
                    at = (slice(k * BLOCK, (k + 1) * BLOCK), slice(j * BLOCK, (j + 1) * BLOCK))
                    out[at] = jnp.zeros((BLOCK, BLOCK), BF16)


def fetch_prune(weight, mask):
    return pl.pallas_call(
        fetch_prune_kernel,
        out_shape=pltpu.VMEM(weight.shape, BF16),
        in_specs=[SCALAR, IN_HBM],
        out_specs=WHOLE,
        scratch_shapes=[pltpu.SemaphoreType.DMA((PIECES,))],
        compiler_params=pltpu.CompilerParams(vmem_limit_bytes=LIMIT),
        cost_estimate=pl.CostEstimate(flops=0, bytes_accessed=1024, transcendentals=0),
        name="prune",
    )(mask, pltpu.with_memory_space_constraint(weight, pltpu.HBM))


def of_core(core, first, second):
    return jnp.where(core == 0, first, second)


def lined(tokens, gate_weight, up_weight, down_weight, gate_mask, up_mask, down_mask):
    core = lax.axis_index("seq")
    weights = []

    def halves(blocks):
        n = len(blocks) // 2
        low, high = jnp.concatenate(blocks[:n]), jnp.concatenate(blocks[n:])
        return of_core(core, high, low), of_core(core, low, high)

    def early(blocks, late):
        gate_w = fetch_prune(gate_weight, gate_mask)
        up_w = fetch_prune(after(up_weight, late['own_y'], late['near_first'], late['pair']), up_mask)
        theirs, mine = halves(blocks)
        return dot(theirs, gate_w), dot(theirs, up_w), mine, gate_w, up_w

    def hidden(mine, gate_w, up_w, gate_in, up_in):
        gate, up = dot(mine, gate_w) + gate_in, dot(mine, up_w) + up_in
        return (jax.nn.silu(gate) * up).astype(BF16)

    def down(mine, theirs, down_w, n):
        low, high = of_core(core, mine, theirs), of_core(core, theirs, mine)
        sums = dot(jnp.concatenate([low, high]), down_w).astype(BF16)
        return jnp.split(sums, n)

    (gate_out, up_out, mine, gate_w, up_w), blocks = gather(tokens, early)
    down_w = prune(after(down_weight, blocks[1]), down_mask)
    first = hidden(mine, gate_w, up_w, swap(gate_out), swap(up_out))
    *blocks, first, down_w = lax.optimization_barrier((*blocks, first, down_w))
    theirs, mine = halves(blocks)
    gate_out, up_out = dot(theirs, gate_w), dot(theirs, up_w)
    second = hidden(mine, gate_w, up_w, swap(gate_out), swap(up_out))
    parts_far = down(second, swap(second), down_w, 4)
    parts_near = down(first, swap(first), down_w, 4)
    return scatter(*parts_near, *parts_far)


def solution(mesh):
    return jax.shard_map(
        lined if mesh.shape["tensor"] == 8 and mesh.shape["seq"] == 2 else plain,
        mesh=mesh,
        in_specs=(
            P(("groups", "tensor"), "seq"),
            P("seq", "tensor"),
            P("seq", "tensor"),
            P("tensor", "seq"),
            P("seq", "tensor"),
            P("seq", "tensor"),
            P("tensor", "seq"),
        ),
        out_specs=P(("groups", "tensor"), "seq"),
        check_vma=False,
    )
```

```python
import jax
import jax.numpy as jnp
from jax import lax
from jax.experimental import pallas as pl
from jax.experimental.pallas import tpu as pltpu
from jax.sharding import PartitionSpec as P

BLOCK = 128
LIMIT = 8 << 20
BF16 = jnp.bfloat16
F32 = jnp.float32


def pruned(weight, mask):
    rows, cols = weight.shape
    shaped = weight.reshape(rows // BLOCK, BLOCK, cols // BLOCK, BLOCK)
    kept = shaped * mask.astype(BF16)[:, None, :, None]
    return kept.reshape(rows, cols)


def dot(a, b):
    return jnp.dot(a, b, preferred_element_type=F32)


def plain(tokens, gate_weight, up_weight, down_weight, gate_mask, up_mask, down_mask):
    gathered = lax.all_gather(tokens, "tensor", axis=0, tiled=True)
    gate_part = dot(gathered, pruned(gate_weight, gate_mask))
    up_part = dot(gathered, pruned(up_weight, up_mask))
    gate = lax.psum_scatter(gate_part, "seq", scatter_dimension=0, tiled=True)
    up = lax.psum_scatter(up_part, "seq", scatter_dimension=0, tiled=True)
    hidden = (jax.nn.silu(gate) * up).astype(BF16)
    full_hidden = lax.all_gather(hidden, "seq", axis=0, tiled=True)
    return lax.psum_scatter(
        dot(full_hidden, pruned(down_weight, down_mask)), "tensor", scatter_dimension=0, tiled=True
    ).astype(BF16)


ACROSS = [(2 * z + y, 2 * z + 1 - y) for z in range(4) for y in range(2)]
PAIR = [(2 * z + y, 2 * (z ^ 1) + y) for z in range(4) for y in range(2)]
MIDDLE = [(2 * z + y, 2 * (3 - z) + y) for z in (1, 2) for y in range(2)]
OUTWARD = [(2 * z + y, 2 * (z ^ 1) + y) for z in (1, 2) for y in range(2)]
INWARD = [(2 * z + y, 2 * (z ^ 1) + y) for z in (0, 3) for y in range(2)]


def move(value, perm):
    return lax.ppermute(value, "tensor", perm)


def inner():
    z = lax.axis_index("tensor") // 2
    return (z == 1) | (z == 2)


def after(value, *others):
    return lax.optimization_barrier((value, *others))[0]


def gather(own, weights):
    pair = move(own, PAIR)
    near_mid = move(own, MIDDLE)
    own_y = move(own, ACROSS)
    gate_w = weights(0)
    far_mid = move(pair, MIDDLE)
    near_out = move(near_mid, PAIR)
    pair_y = move(after(pair, own_y), ACROSS)
    up_w = weights(1, own_y, near_mid, pair)
    near = jnp.where(inner(), near_mid, near_out)
    far_out = move(far_mid, PAIR)
    near_y = move(after(near, pair_y), ACROSS)
    down_w = weights(2, near, pair_y)
    far = jnp.where(inner(), far_mid, far_out)
    far, near_y, gate_w, up_w, down_w = lax.optimization_barrier((far, near_y, gate_w, up_w, down_w))
    far_y = move(far, ACROSS)
    return (own, own_y, pair, pair_y, near, near_y), (far, far_y), (gate_w, up_w, down_w)


def add(a, b):
    return a.astype(F32) + b.astype(F32)


def scatter(own, own_y, pair, pair_y, near, near_y, far, far_y):
    far_in = move(far_y, ACROSS)
    near_in = move(near_y, ACROSS)
    pair_in = move(after(pair_y, near_in), ACROSS)
    own_in = move(after(own_y, near_in), ACROSS)
    far_s = add(after(far, near), far_in).astype(BF16)
    near_s = add(after(near, far_s), near_in).astype(BF16)
    far_s = add(far_s, move(far_s, PAIR)).astype(BF16)
    near_s = add(near_s, move(near_s, PAIR)).astype(BF16)
    pair_s = (add(pair, pair_in) + move(far_s, MIDDLE).astype(F32)).astype(BF16)
    own_s = add(own, own_in) + move(near_s, MIDDLE).astype(F32)
    return add(own_s, move(pair_s, PAIR)).astype(BF16)


SWAP = [(0, 1), (1, 0)]
WHOLE = pl.BlockSpec(memory_space=pltpu.VMEM)
IN_HBM = pl.BlockSpec(memory_space=pltpu.HBM)
PIECES = 8
SCALAR = pl.BlockSpec(memory_space=pltpu.SMEM)


def swap(value):
    return lax.ppermute(value, "seq", SWAP)


def prune_kernel(mask, weight, out, arrived):
    rows = out.shape[0] // PIECES
    copies = [
        pltpu.make_async_copy(
            weight.at[pl.ds(i * rows, rows), :], out.at[pl.ds(i * rows, rows), :], arrived.at[i]
        )
        for i in range(PIECES)
    ]
    for copy in copies:
        copy.start()
    for i, copy in enumerate(copies):
        copy.wait()
        for k in range(i * rows // BLOCK, (i + 1) * rows // BLOCK):
            for j in range(out.shape[1] // BLOCK):

                @pl.when(mask[k, j] == 0)
                def _():
                    at = (slice(k * BLOCK, (k + 1) * BLOCK), slice(j * BLOCK, (j + 1) * BLOCK))
                    out[at] = jnp.zeros((BLOCK, BLOCK), BF16)


def prune(weight, mask):
    return pl.pallas_call(
        prune_kernel,
        out_shape=pltpu.VMEM(weight.shape, BF16),
        in_specs=[SCALAR, IN_HBM],
        out_specs=WHOLE,
        scratch_shapes=[pltpu.SemaphoreType.DMA((PIECES,))],
        compiler_params=pltpu.CompilerParams(vmem_limit_bytes=LIMIT),
        cost_estimate=pl.CostEstimate(flops=0, bytes_accessed=1024, transcendentals=0),
        name="prune",
    )(mask, pltpu.with_memory_space_constraint(weight, pltpu.HBM))


def of_core(core, first, second):
    return jnp.where(core == 0, first, second)


def halves(core, blocks):
    n = len(blocks) // 2
    low, high = jnp.concatenate(blocks[:n]), jnp.concatenate(blocks[n:])
    return of_core(core, high, low), of_core(core, low, high)


def down(core, mine, theirs, down_w, n):
    low, high = of_core(core, mine, theirs), of_core(core, theirs, mine)
    return jnp.split(dot(jnp.concatenate([low, high]), down_w).astype(BF16), n)


def activated(gate, up):
    return (jax.nn.silu(gate) * up).astype(BF16)


def lined(tokens, gate_weight, up_weight, down_weight, gate_mask, up_mask, down_mask):
    core = lax.axis_index("seq")
    stored = ((gate_weight, gate_mask), (up_weight, up_mask), (down_weight, down_mask))

    def weights(i, *others):
        weight, mask = stored[i]
        return prune(after(weight, *others) if others else weight, mask)

    first, last, (gate_w, up_w, down_w) = gather(tokens, weights)
    theirs, mine = halves(core, first)
    gate_out, up_out = dot(theirs, gate_w), dot(theirs, up_w)
    gate_in, up_in = swap(gate_out), swap(up_out)

    last = (last[0], after(last[1], gate_out, up_out))
    last_theirs, last_mine = halves(core, last)
    rows = last_mine.shape[0]
    last_rows = jnp.concatenate([last_theirs, last_mine])
    last_gate, last_up = dot(last_rows, gate_w), dot(last_rows, up_w)
    last_gate_in, last_up_in = swap(last_gate[:rows]), swap(last_up[:rows])
    gate = dot(after(mine, last_gate, last_up), gate_w) + gate_in
    last_hidden = activated(last_gate[rows:] + last_gate_in, last_up[rows:] + after(last_up_in, gate))
    hidden = activated(gate, dot(after(mine, last_hidden), up_w) + up_in)

    last_parts = down(core, last_hidden, after(swap(last_hidden), hidden), down_w, 2)
    parts = down(core, hidden, swap(hidden), down_w, 6)
    return scatter(*parts, *last_parts)


def solution(mesh):
    return jax.shard_map(
        lined if mesh.shape["tensor"] == 8 and mesh.shape["seq"] == 2 else plain,
        mesh=mesh,
        in_specs=(
            P(("groups", "tensor"), "seq"),
            P("seq", "tensor"),
            P("seq", "tensor"),
            P("tensor", "seq"),
            P("seq", "tensor"),
            P("seq", "tensor"),
            P("tensor", "seq"),
        ),
        out_specs=P(("groups", "tensor"), "seq"),
        check_vma=False,
    )
```

```python
import jax
import jax.numpy as jnp
from jax import lax
from jax.experimental import pallas as pl
from jax.experimental.pallas import tpu as pltpu
from jax.sharding import PartitionSpec as P

BLOCK = 128
LIMIT = 8 << 20
BF16 = jnp.bfloat16
F32 = jnp.float32


def pruned(weight, mask):
    rows, cols = weight.shape
    shaped = weight.reshape(rows // BLOCK, BLOCK, cols // BLOCK, BLOCK)
    kept = shaped * mask.astype(BF16)[:, None, :, None]
    return kept.reshape(rows, cols)


def dot(a, b):
    return jnp.dot(a, b, preferred_element_type=F32)


def plain(tokens, gate_weight, up_weight, down_weight, gate_mask, up_mask, down_mask):
    gathered = lax.all_gather(tokens, "tensor", axis=0, tiled=True)
    gate_part = dot(gathered, pruned(gate_weight, gate_mask))
    up_part = dot(gathered, pruned(up_weight, up_mask))
    gate = lax.psum_scatter(gate_part, "seq", scatter_dimension=0, tiled=True)
    up = lax.psum_scatter(up_part, "seq", scatter_dimension=0, tiled=True)
    hidden = (jax.nn.silu(gate) * up).astype(BF16)
    full_hidden = lax.all_gather(hidden, "seq", axis=0, tiled=True)
    return lax.psum_scatter(
        dot(full_hidden, pruned(down_weight, down_mask)), "tensor", scatter_dimension=0, tiled=True
    ).astype(BF16)


ACROSS = [(2 * z + y, 2 * z + 1 - y) for z in range(4) for y in range(2)]
PAIR = [(2 * z + y, 2 * (z ^ 1) + y) for z in range(4) for y in range(2)]
MIDDLE = [(2 * z + y, 2 * (3 - z) + y) for z in (1, 2) for y in range(2)]
OUTWARD = [(2 * z + y, 2 * (z ^ 1) + y) for z in (1, 2) for y in range(2)]
INWARD = [(2 * z + y, 2 * (z ^ 1) + y) for z in (0, 3) for y in range(2)]


def move(value, perm):
    return lax.ppermute(value, "tensor", perm)


def inner():
    z = lax.axis_index("tensor") // 2
    return (z == 1) | (z == 2)


def after(value, *others):
    return lax.optimization_barrier((value, *others))[0]


def gather(own, weights):
    pair = move(own, PAIR)
    near_mid = move(own, MIDDLE)
    own_y = move(own, ACROSS)
    gate_w = weights(0)
    far_mid = move(pair, MIDDLE)
    near_out = move(near_mid, PAIR)
    pair_y = move(after(pair, own_y), ACROSS)
    up_w = weights(1, own_y, near_mid, pair)
    near = jnp.where(inner(), near_mid, near_out)
    far_out = move(far_mid, PAIR)
    near_y = move(after(near, pair_y), ACROSS)
    down_w = weights(2, near, pair_y)
    far = jnp.where(inner(), far_mid, far_out)
    far, near_y, gate_w, up_w, down_w = lax.optimization_barrier((far, near_y, gate_w, up_w, down_w))
    far_y = move(far, ACROSS)
    return (own, own_y, pair, pair_y, near, near_y), (far, far_y), (gate_w, up_w, down_w)


def add(a, b):
    return a.astype(F32) + b.astype(F32)


def scatter(own, own_y, pair, pair_y, near, near_y, far, far_y):
    far_in = move(far_y, ACROSS)
    near_in = move(near_y, ACROSS)
    far_s = add(after(far, near), far_in).astype(BF16)
    far_t = add(far_s, move(far_s, PAIR)).astype(BF16)
    near_s = add(after(near, far_s), near_in).astype(BF16)
    pair_in = move(after(pair_y, far_s), ACROSS)
    near_t = add(near_s, move(near_s, PAIR)).astype(BF16)
    own_in = move(after(own_y, far_t), ACROSS)
    pair_s = (add(pair, pair_in) + move(far_t, MIDDLE).astype(F32)).astype(BF16)
    own_s = add(own, own_in) + move(near_t, MIDDLE).astype(F32)
    return add(own_s, move(pair_s, PAIR)).astype(BF16)


SWAP = [(0, 1), (1, 0)]
WHOLE = pl.BlockSpec(memory_space=pltpu.VMEM)
IN_HBM = pl.BlockSpec(memory_space=pltpu.HBM)
PIECES = 8
SCALAR = pl.BlockSpec(memory_space=pltpu.SMEM)


def swap(value):
    return lax.ppermute(value, "seq", SWAP)


def prune_kernel(mask, weight, out, arrived):
    rows = out.shape[0] // PIECES
    copies = [
        pltpu.make_async_copy(
            weight.at[pl.ds(i * rows, rows), :], out.at[pl.ds(i * rows, rows), :], arrived.at[i]
        )
        for i in range(PIECES)
    ]
    for copy in copies:
        copy.start()
    for i, copy in enumerate(copies):
        copy.wait()
        for k in range(i * rows // BLOCK, (i + 1) * rows // BLOCK):
            for j in range(out.shape[1] // BLOCK):

                @pl.when(mask[k, j] == 0)
                def _():
                    at = (slice(k * BLOCK, (k + 1) * BLOCK), slice(j * BLOCK, (j + 1) * BLOCK))
                    out[at] = jnp.zeros((BLOCK, BLOCK), BF16)


def prune(weight, mask):
    return pl.pallas_call(
        prune_kernel,
        out_shape=pltpu.VMEM(weight.shape, BF16),
        in_specs=[SCALAR, IN_HBM],
        out_specs=WHOLE,
        scratch_shapes=[pltpu.SemaphoreType.DMA((PIECES,))],
        compiler_params=pltpu.CompilerParams(vmem_limit_bytes=LIMIT),
        cost_estimate=pl.CostEstimate(flops=0, bytes_accessed=1024, transcendentals=0),
        name="prune",
    )(mask, pltpu.with_memory_space_constraint(weight, pltpu.HBM))


def of_core(core, first, second):
    return jnp.where(core == 0, first, second)


def halves(core, blocks):
    n = len(blocks) // 2
    low, high = jnp.concatenate(blocks[:n]), jnp.concatenate(blocks[n:])
    return of_core(core, high, low), of_core(core, low, high)


def down(core, mine, theirs, down_w, n):
    low, high = of_core(core, mine, theirs), of_core(core, theirs, mine)
    return jnp.split(dot(jnp.concatenate([low, high]), down_w).astype(BF16), n)


def activated(gate, up):
    return (jax.nn.silu(gate) * up).astype(BF16)


def lined(tokens, gate_weight, up_weight, down_weight, gate_mask, up_mask, down_mask):
    core = lax.axis_index("seq")
    stored = ((gate_weight, gate_mask), (up_weight, up_mask), (down_weight, down_mask))

    def weights(i, *others):
        weight, mask = stored[i]
        return prune(after(weight, *others) if others else weight, mask)

    first, last, (gate_w, up_w, down_w) = gather(tokens, weights)
    theirs, mine = halves(core, first)
    gate_out, up_out = dot(theirs, gate_w), dot(theirs, up_w)
    gate_in, up_in = swap(gate_out), swap(up_out)

    last = (last[0], after(last[1], gate_out, up_out))
    last_theirs, last_mine = halves(core, last)
    rows = last_mine.shape[0]
    last_rows = jnp.concatenate([last_theirs, last_mine])
    last_gate, last_up = dot(last_rows, gate_w), dot(last_rows, up_w)
    last_gate_in, last_up_in = swap(last_gate[:rows]), swap(last_up[:rows])
    gate = dot(after(mine, last_gate, last_up), gate_w) + gate_in
    last_hidden = activated(last_gate[rows:] + last_gate_in, last_up[rows:] + after(last_up_in, gate))
    hidden = activated(gate, dot(after(mine, last_hidden), up_w) + up_in)

    last_parts = down(core, last_hidden, after(swap(last_hidden), hidden), down_w, 2)
    parts = down(core, hidden, swap(hidden), down_w, 6)
    return scatter(*parts, *last_parts)


def solution(mesh):
    return jax.shard_map(
        lined if mesh.shape["tensor"] == 8 and mesh.shape["seq"] == 2 else plain,
        mesh=mesh,
        in_specs=(
            P(("groups", "tensor"), "seq"),
            P("seq", "tensor"),
            P("seq", "tensor"),
            P("tensor", "seq"),
            P("seq", "tensor"),
            P("seq", "tensor"),
            P("tensor", "seq"),
        ),
        out_specs=P(("groups", "tensor"), "seq"),
        check_vma=False,
    )
```

```python
import jax
import jax.numpy as jnp
from jax import lax
from jax.experimental import pallas as pl
from jax.experimental.pallas import tpu as pltpu
from jax.sharding import PartitionSpec as P

BLOCK = 128
LIMIT = 8 << 20
BF16 = jnp.bfloat16
F32 = jnp.float32


def pruned(weight, mask):
    rows, cols = weight.shape
    shaped = weight.reshape(rows // BLOCK, BLOCK, cols // BLOCK, BLOCK)
    kept = shaped * mask.astype(BF16)[:, None, :, None]
    return kept.reshape(rows, cols)


def dot(a, b):
    return jnp.dot(a, b, preferred_element_type=F32)


def plain(tokens, gate_weight, up_weight, down_weight, gate_mask, up_mask, down_mask):
    gathered = lax.all_gather(tokens, "tensor", axis=0, tiled=True)
    gate_part = dot(gathered, pruned(gate_weight, gate_mask))
    up_part = dot(gathered, pruned(up_weight, up_mask))
    gate = lax.psum_scatter(gate_part, "seq", scatter_dimension=0, tiled=True)
    up = lax.psum_scatter(up_part, "seq", scatter_dimension=0, tiled=True)
    hidden = (jax.nn.silu(gate) * up).astype(BF16)
    full_hidden = lax.all_gather(hidden, "seq", axis=0, tiled=True)
    return lax.psum_scatter(
        dot(full_hidden, pruned(down_weight, down_mask)), "tensor", scatter_dimension=0, tiled=True
    ).astype(BF16)


ACROSS = [(2 * z + y, 2 * z + 1 - y) for z in range(4) for y in range(2)]
PAIR = [(2 * z + y, 2 * (z ^ 1) + y) for z in range(4) for y in range(2)]
MIDDLE = [(2 * z + y, 2 * (3 - z) + y) for z in (1, 2) for y in range(2)]
OUTWARD = [(2 * z + y, 2 * (z ^ 1) + y) for z in (1, 2) for y in range(2)]
INWARD = [(2 * z + y, 2 * (z ^ 1) + y) for z in (0, 3) for y in range(2)]


def move(value, perm):
    return lax.ppermute(value, "tensor", perm)


def inner():
    z = lax.axis_index("tensor") // 2
    return (z == 1) | (z == 2)


def after(value, *others):
    return lax.optimization_barrier((value, *others))[0]


def gather(own, weights):
    pair = move(own, PAIR)
    near_mid = move(own, MIDDLE)
    own_y = move(own, ACROSS)
    gate_w = weights(0)
    far_mid = move(pair, MIDDLE)
    near_out = move(near_mid, PAIR)
    pair_y = move(after(pair, own_y), ACROSS)
    up_w = weights(1, own_y, near_mid, pair)
    near = jnp.where(inner(), near_mid, near_out)
    far_out = move(far_mid, PAIR)
    near_y = move(after(near, pair_y), ACROSS)
    down_w = weights(2, near, pair_y)
    far = jnp.where(inner(), far_mid, far_out)
    far, near_y, gate_w, up_w, down_w = lax.optimization_barrier((far, near_y, gate_w, up_w, down_w))
    far_y = move(far, ACROSS)
    return (own, own_y, pair, pair_y, near, near_y), (far, far_y), (gate_w, up_w, down_w)


def add(a, b):
    return a.astype(F32) + b.astype(F32)


def scatter(own, own_y, pair, pair_y, near, near_y, far, far_y):
    far_in = move(far_y, ACROSS)
    near_in = move(near_y, ACROSS)
    far_s = add(after(far, near), far_in).astype(BF16)
    far_t = add(far_s, move(far_s, PAIR)).astype(BF16)
    near_s = add(after(near, far_s), near_in).astype(BF16)
    pair_in = move(after(pair_y, far_s), ACROSS)
    near_t = add(near_s, move(near_s, PAIR)).astype(BF16)
    own_in = move(after(own_y, far_t), ACROSS)
    pair_s = (add(pair, pair_in) + move(far_t, MIDDLE).astype(F32)).astype(BF16)
    own_s = add(own, own_in) + move(near_t, MIDDLE).astype(F32)
    return add(own_s, move(pair_s, PAIR)).astype(BF16)


SWAP = [(0, 1), (1, 0)]
WHOLE = pl.BlockSpec(memory_space=pltpu.VMEM)
IN_HBM = pl.BlockSpec(memory_space=pltpu.HBM)
PIECES = 8
SCALAR = pl.BlockSpec(memory_space=pltpu.SMEM)


def swap(value):
    return lax.ppermute(value, "seq", SWAP)


def prune_kernel(mask, weight, out, arrived):
    rows = out.shape[0] // PIECES
    copies = [
        pltpu.make_async_copy(
            weight.at[pl.ds(i * rows, rows), :], out.at[pl.ds(i * rows, rows), :], arrived.at[i]
        )
        for i in range(PIECES)
    ]
    for copy in copies:
        copy.start()
    for i, copy in enumerate(copies):
        copy.wait()
        for k in range(i * rows // BLOCK, (i + 1) * rows // BLOCK):
            for j in range(out.shape[1] // BLOCK):

                @pl.when(mask[k, j] == 0)
                def _():
                    at = (slice(k * BLOCK, (k + 1) * BLOCK), slice(j * BLOCK, (j + 1) * BLOCK))
                    out[at] = jnp.zeros((BLOCK, BLOCK), BF16)


def prune(weight, mask):
    return pl.pallas_call(
        prune_kernel,
        out_shape=pltpu.VMEM(weight.shape, BF16),
        in_specs=[SCALAR, IN_HBM],
        out_specs=WHOLE,
        scratch_shapes=[pltpu.SemaphoreType.DMA((PIECES,))],
        compiler_params=pltpu.CompilerParams(vmem_limit_bytes=LIMIT),
        cost_estimate=pl.CostEstimate(flops=0, bytes_accessed=1024, transcendentals=0),
        name="prune",
    )(mask, pltpu.with_memory_space_constraint(weight, pltpu.HBM))


def copy_kernel(mask, weight, out):
    for k in range(out.shape[0] // BLOCK):
        for j in range(out.shape[1] // BLOCK):
            at = (slice(k * BLOCK, (k + 1) * BLOCK), slice(j * BLOCK, (j + 1) * BLOCK))

            @pl.when(mask[k, j] != 0)
            def _():
                out[at] = weight[at]

            @pl.when(mask[k, j] == 0)
            def _():
                out[at] = jnp.zeros((BLOCK, BLOCK), BF16)


def prune_fetched(weight, mask):
    return pl.pallas_call(
        copy_kernel,
        out_shape=pltpu.VMEM(weight.shape, BF16),
        in_specs=[SCALAR, WHOLE],
        out_specs=WHOLE,
        compiler_params=pltpu.CompilerParams(vmem_limit_bytes=LIMIT),
        cost_estimate=pl.CostEstimate(flops=0, bytes_accessed=1024, transcendentals=0),
        name="prune_fetched",
    )(mask, weight)


def of_core(core, first, second):
    return jnp.where(core == 0, first, second)


def halves(core, blocks):
    n = len(blocks) // 2
    low, high = jnp.concatenate(blocks[:n]), jnp.concatenate(blocks[n:])
    return of_core(core, high, low), of_core(core, low, high)


def down(core, mine, theirs, down_w, n):
    low, high = of_core(core, mine, theirs), of_core(core, theirs, mine)
    return jnp.split(dot(jnp.concatenate([low, high]), down_w).astype(BF16), n)


def activated(gate, up):
    return (jax.nn.silu(gate) * up).astype(BF16)


def lined(tokens, gate_weight, up_weight, down_weight, gate_mask, up_mask, down_mask):
    core = lax.axis_index("seq")
    stored = ((gate_weight, gate_mask), (up_weight, up_mask), (down_weight, down_mask))

    def weights(i, *others):
        weight, mask = stored[i]
        return (prune_fetched if i == 2 else prune)(after(weight, *others) if others else weight, mask)

    first, last, (gate_w, up_w, down_w) = gather(tokens, weights)
    theirs, mine = halves(core, first)
    gate_out, up_out = dot(theirs, gate_w), dot(theirs, up_w)
    gate_in, up_in = swap(gate_out), swap(up_out)

    last = (last[0], after(last[1], gate_out, up_out))
    last_theirs, last_mine = halves(core, last)
    rows = last_mine.shape[0]
    last_rows = jnp.concatenate([last_theirs, last_mine])
    last_gate, last_up = dot(last_rows, gate_w), dot(last_rows, up_w)
    last_gate_in, last_up_in = swap(last_gate[:rows]), swap(last_up[:rows])
    gate = dot(after(mine, last_gate, last_up), gate_w) + gate_in
    last_hidden = activated(last_gate[rows:] + last_gate_in, last_up[rows:] + after(last_up_in, gate))
    hidden = activated(gate, dot(after(mine, last_hidden), up_w) + up_in)

    last_parts = down(core, last_hidden, after(swap(last_hidden), hidden), down_w, 2)
    parts = down(core, hidden, swap(hidden), down_w, 6)
    return scatter(*parts, *last_parts)


def solution(mesh):
    return jax.shard_map(
        lined if mesh.shape["tensor"] == 8 and mesh.shape["seq"] == 2 else plain,
        mesh=mesh,
        in_specs=(
            P(("groups", "tensor"), "seq"),
            P("seq", "tensor"),
            P("seq", "tensor"),
            P("tensor", "seq"),
            P("seq", "tensor"),
            P("seq", "tensor"),
            P("tensor", "seq"),
        ),
        out_specs=P(("groups", "tensor"), "seq"),
        check_vma=False,
    )
```

```python
import jax
import jax.numpy as jnp
from jax import lax
from jax.experimental import pallas as pl
from jax.experimental.pallas import tpu as pltpu
from jax.sharding import PartitionSpec as P

BLOCK = 128
LIMIT = 8 << 20
BF16 = jnp.bfloat16
F32 = jnp.float32


def pruned(weight, mask):
    rows, cols = weight.shape
    shaped = weight.reshape(rows // BLOCK, BLOCK, cols // BLOCK, BLOCK)
    kept = shaped * mask.astype(BF16)[:, None, :, None]
    return kept.reshape(rows, cols)


def dot(a, b):
    return jnp.dot(a, b, preferred_element_type=F32)


def plain(tokens, gate_weight, up_weight, down_weight, gate_mask, up_mask, down_mask):
    gathered = lax.all_gather(tokens, "tensor", axis=0, tiled=True)
    gate_part = dot(gathered, pruned(gate_weight, gate_mask))
    up_part = dot(gathered, pruned(up_weight, up_mask))
    gate = lax.psum_scatter(gate_part, "seq", scatter_dimension=0, tiled=True)
    up = lax.psum_scatter(up_part, "seq", scatter_dimension=0, tiled=True)
    hidden = (jax.nn.silu(gate) * up).astype(BF16)
    full_hidden = lax.all_gather(hidden, "seq", axis=0, tiled=True)
    return lax.psum_scatter(
        dot(full_hidden, pruned(down_weight, down_mask)), "tensor", scatter_dimension=0, tiled=True
    ).astype(BF16)


ACROSS = [(2 * z + y, 2 * z + 1 - y) for z in range(4) for y in range(2)]
PAIR = [(2 * z + y, 2 * (z ^ 1) + y) for z in range(4) for y in range(2)]
MIDDLE = [(2 * z + y, 2 * (3 - z) + y) for z in (1, 2) for y in range(2)]
OUTWARD = [(2 * z + y, 2 * (z ^ 1) + y) for z in (1, 2) for y in range(2)]
INWARD = [(2 * z + y, 2 * (z ^ 1) + y) for z in (0, 3) for y in range(2)]


def move(value, perm):
    return lax.ppermute(value, "tensor", perm)


def inner():
    z = lax.axis_index("tensor") // 2
    return (z == 1) | (z == 2)


def after(value, *others):
    return lax.optimization_barrier((value, *others))[0]


def gather(own, weights):
    pair = move(own, PAIR)
    near_mid = move(own, MIDDLE)
    own_y = move(own, ACROSS)
    gate_w = weights(0)
    far_mid = move(pair, MIDDLE)
    near_out = move(near_mid, OUTWARD)
    pair_y = move(after(pair, own_y), ACROSS)
    up_w = weights(1, own_y, near_mid, pair)
    near = jnp.where(inner(), near_mid, near_out)
    far_out = move(far_mid, OUTWARD)
    near_y = move(after(near, pair_y), ACROSS)
    down_w = weights(2, near, pair_y)
    far = jnp.where(inner(), far_mid, far_out)
    far, near_y, gate_w, up_w, down_w = lax.optimization_barrier((far, near_y, gate_w, up_w, down_w))
    far_y = move(far, ACROSS)
    return (own, own_y, pair, pair_y, near, near_y), (far, far_y), (gate_w, up_w, down_w)


def add(a, b):
    return a.astype(F32) + b.astype(F32)


def scatter(own, own_y, pair, pair_y, near, near_y, far, far_y):
    far_in = move(far_y, ACROSS)
    near_in = move(near_y, ACROSS)
    far_s = add(after(far, near), far_in).astype(BF16)
    far_t = add(far_s, move(far_s, PAIR)).astype(BF16)
    near_s = add(after(near, far_s), near_in).astype(BF16)
    pair_in = move(after(pair_y, far_s), ACROSS)
    near_t = add(near_s, move(near_s, PAIR)).astype(BF16)
    own_in = move(after(own_y, far_t), ACROSS)
    pair_s = (add(pair, pair_in) + move(far_t, MIDDLE).astype(F32)).astype(BF16)
    own_s = add(own, own_in) + move(near_t, MIDDLE).astype(F32)
    return add(own_s, move(pair_s, PAIR)).astype(BF16)


SWAP = [(0, 1), (1, 0)]
WHOLE = pl.BlockSpec(memory_space=pltpu.VMEM)
IN_HBM = pl.BlockSpec(memory_space=pltpu.HBM)
PIECES = 8
SCALAR = pl.BlockSpec(memory_space=pltpu.SMEM)


def swap(value):
    return lax.ppermute(value, "seq", SWAP)


def prune_kernel(mask, weight, out, arrived):
    rows = out.shape[0] // PIECES
    copies = [
        pltpu.make_async_copy(
            weight.at[pl.ds(i * rows, rows), :], out.at[pl.ds(i * rows, rows), :], arrived.at[i]
        )
        for i in range(PIECES)
    ]
    for copy in copies:
        copy.start()
    for i, copy in enumerate(copies):
        copy.wait()
        for k in range(i * rows // BLOCK, (i + 1) * rows // BLOCK):
            for j in range(out.shape[1] // BLOCK):

                @pl.when(mask[k, j] == 0)
                def _():
                    at = (slice(k * BLOCK, (k + 1) * BLOCK), slice(j * BLOCK, (j + 1) * BLOCK))
                    out[at] = jnp.zeros((BLOCK, BLOCK), BF16)


def prune(weight, mask):
    return pl.pallas_call(
        prune_kernel,
        out_shape=pltpu.VMEM(weight.shape, BF16),
        in_specs=[SCALAR, IN_HBM],
        out_specs=WHOLE,
        scratch_shapes=[pltpu.SemaphoreType.DMA((PIECES,))],
        compiler_params=pltpu.CompilerParams(vmem_limit_bytes=LIMIT),
        cost_estimate=pl.CostEstimate(flops=0, bytes_accessed=1024, transcendentals=0),
        name="prune",
    )(mask, pltpu.with_memory_space_constraint(weight, pltpu.HBM))


def copy_kernel(mask, weight, out):
    for k in range(out.shape[0] // BLOCK):
        for j in range(out.shape[1] // BLOCK):
            at = (slice(k * BLOCK, (k + 1) * BLOCK), slice(j * BLOCK, (j + 1) * BLOCK))

            @pl.when(mask[k, j] != 0)
            def _():
                out[at] = weight[at]

            @pl.when(mask[k, j] == 0)
            def _():
                out[at] = jnp.zeros((BLOCK, BLOCK), BF16)


def prune_fetched(weight, mask):
    return pl.pallas_call(
        copy_kernel,
        out_shape=pltpu.VMEM(weight.shape, BF16),
        in_specs=[SCALAR, WHOLE],
        out_specs=WHOLE,
        compiler_params=pltpu.CompilerParams(vmem_limit_bytes=LIMIT),
        cost_estimate=pl.CostEstimate(flops=0, bytes_accessed=1024, transcendentals=0),
        name="prune_fetched",
    )(mask, weight)


def of_core(core, first, second):
    return jnp.where(core == 0, first, second)


def halves(core, blocks):
    n = len(blocks) // 2
    low, high = jnp.concatenate(blocks[:n]), jnp.concatenate(blocks[n:])
    return of_core(core, high, low), of_core(core, low, high)


def down(core, mine, theirs, down_w, n):
    low, high = of_core(core, mine, theirs), of_core(core, theirs, mine)
    return jnp.split(dot(jnp.concatenate([low, high]), down_w).astype(BF16), n)


def activated(gate, up):
    return (jax.nn.silu(gate) * up).astype(BF16)


def lined(tokens, gate_weight, up_weight, down_weight, gate_mask, up_mask, down_mask):
    core = lax.axis_index("seq")
    stored = ((gate_weight, gate_mask), (up_weight, up_mask), (down_weight, down_mask))

    def weights(i, *others):
        weight, mask = stored[i]
        return (prune_fetched if i == 2 else prune)(after(weight, *others) if others else weight, mask)

    first, last, (gate_w, up_w, down_w) = gather(tokens, weights)
    theirs, mine = halves(core, first)
    gate_out, up_out = dot(theirs, gate_w), dot(theirs, up_w)
    gate_in, up_in = swap(gate_out), swap(up_out)

    last = (last[0], after(last[1], gate_out, up_out))
    last_theirs, last_mine = halves(core, last)
    rows = last_mine.shape[0]
    last_rows = jnp.concatenate([last_theirs, last_mine])
    last_gate, last_up = dot(last_rows, gate_w), dot(last_rows, up_w)
    last_gate_in, last_up_in = swap(last_gate[:rows]), swap(last_up[:rows])
    gate = dot(after(mine, last_gate, last_up), gate_w) + gate_in
    last_hidden = activated(last_gate[rows:] + last_gate_in, last_up[rows:] + after(last_up_in, gate))
    hidden = activated(gate, dot(after(mine, last_hidden), up_w) + up_in)

    last_parts = down(core, last_hidden, after(swap(last_hidden), hidden), down_w, 2)
    parts = down(core, hidden, swap(hidden), down_w, 6)
    return scatter(*parts, *last_parts)


def solution(mesh):
    return jax.shard_map(
        lined if mesh.shape["tensor"] == 8 and mesh.shape["seq"] == 2 else plain,
        mesh=mesh,
        in_specs=(
            P(("groups", "tensor"), "seq"),
            P("seq", "tensor"),
            P("seq", "tensor"),
            P("tensor", "seq"),
            P("seq", "tensor"),
            P("seq", "tensor"),
            P("tensor", "seq"),
        ),
        out_specs=P(("groups", "tensor"), "seq"),
        check_vma=False,
    )
```
